512 devices in a mesh: row: 8 (over y, core), col: 8 (over x, z_hi), fsdp: 8 (over z_lo).
Axes of the slice: x: 4, y: 4, z: 16 (z_hi: 2, z_lo: 8; z = z_hi * 8 + z_lo), core: 2. Of those that a mesh axis runs over, the one named last changes fastest.
Arguments:
- master: float32 [8, 8, 192, 4096], P('row', 'col', 'fsdp'), may hold values from -6 to 6
- moment_one: float32 [8, 8, 192, 4096], P('row', 'col', 'fsdp'), may hold values from -3 to 3
- moment_two: float32 [8, 8, 192, 4096], P('row', 'col', 'fsdp'), may hold values from 0.01 to 1
- grads: bfloat16 [8, 8, 192, 4096], P('row', 'col', 'fsdp'), may hold values from -6 to 6
- counts: int32 [8, 8, 8], P('row', 'col'), may hold values from 1 to 4095
- step: int32 [1], replicated, may hold values from 1 to 15
Outputs:
- new_master: float32 [8, 8, 192, 4096], P('row', 'col', 'fsdp')
- new_moment_one: float32 [8, 8, 192, 4096], P('row', 'col', 'fsdp')
- new_moment_two: float32 [8, 8, 192, 4096], P('row', 'col', 'fsdp')
- replica_weights: bfloat16 [8, 8, 8, 192, 4096], P('row', 'col', 'fsdp')
The draws below stay inside these ranges and needn't reach their ends.
All inputs are finite; a program needn't handle non-finite values.
Results may differ from the reference program's by a relative error of at most 0.001.
Values may be sent and summed in bfloat16 or wider, within the bound.
A program may use at most 64 MiB of HBM per device.

```python
import math
import jax
import jax.numpy as jnp
from jax import lax

D = 4096
BUCKETS = 8
ROWS = 192
N_ROW = 8
N_COL = 8
N_FSDP = 8


def place_ends(entries, own_key, smallest, largest):
    place = [jax.random.randint(jax.random.fold_in(own_key, axis), (), 0, length) for axis, length in enumerate(entries.shape)]
    main_axis = entries.shape.index(max(entries.shape))
    next_to = place[:main_axis] + [(place[main_axis] + 1) % entries.shape[main_axis]] + place[main_axis + 1:]
    return entries.at[tuple(place)].set(smallest).at[tuple(next_to)].set(largest)


def level_of(own_key, shape, pieces, low, largest):
    def one(dim, shards_of):
        steps = jax.random.uniform(jax.random.fold_in(jax.random.fold_in(own_key, 6), dim), (shards_of,), jnp.float32, low / len(pieces), largest / len(pieces))
        return jnp.repeat(jnp.exp(steps), shape[dim] // shards_of).reshape((-1,) + (1,) * (len(shape) - dim - 1))

    loudness = one(*pieces[0])
    for cut in pieces[1:]:
        loudness = loudness * one(*cut)
    return loudness


def scatter_about(own_key, extent, scale, most, cuts=(), kind=jnp.bfloat16):
    entries = jax.random.normal(own_key, extent, jnp.float32) * scale
    if len(cuts) > 0:
        entries = level_of(own_key, extent, cuts, -0.22, 0.18) * entries
    return jnp.clip(entries, min=-most, max=most).astype(kind)


def setup_inputs(seed: int = 0) -> dict:
    key_list = jax.random.split(jax.random.key(seed), 7)
    return {
        "master": scatter_about(key_list[0], (N_ROW, N_COL, ROWS, D), 1.0, 6.0, ((0, 8), (1, 8), (2, 8)), jnp.float32),
        "moment_one": scatter_about(key_list[1], (N_ROW, N_COL, ROWS, D), 0.3, 3.0, ((0, 8), (1, 8), (2, 8)), jnp.float32),
        "moment_two": jnp.clip(jnp.exp(math.log(1.0) - 4.6051702 * jax.random.uniform(key_list[2], (N_ROW, N_COL, ROWS, D), jnp.float32) ** level_of(key_list[2], (N_ROW, N_COL, ROWS, D), ((0, 8), (1, 8), (2, 8)), -0.2, 0.2)), 0.01, 1.0),
        "grads": scatter_about(key_list[3], (N_ROW, N_COL, ROWS, D), 1.0, 6.0, ((0, 8), (1, 8), (2, 8))),
        "counts": place_ends(jax.random.randint(key_list[4], (N_ROW, N_COL, BUCKETS), 1, 4096), jax.random.fold_in(key_list[4], 1), 1, 4095).astype(jnp.int32),
        "step": jax.random.randint(key_list[5], (1,), 1, 16).astype(jnp.int32),
    }


def token_mass(counts):
    lengths = 256.0 * jnp.power(2.0, jnp.arange(BUCKETS).astype(jnp.float32))
    return lax.optimization_barrier(jnp.sum(counts.astype(jnp.float32) * lengths, axis=-1))

def cycle_round(states, weight, axis):
    total = jnp.roll(weight, 1, axis) + weight + jnp.roll(weight, -1, axis)
    scaled_weight = weight[:, :, None, None]
    scaled_total = total[:, :, None, None]
    result = []
    for state in states:
        weighted = scaled_weight * state
        summed = jnp.roll(weighted, 1, axis) + weighted + jnp.roll(weighted, -1, axis)
        result.append(summed / scaled_total)
    return (result, total / 3.0)

def reference(master, moment_one, moment_two, grads, counts, step):
    steps_f = step[0].astype(jnp.float32)
    grad_f = grads.astype(jnp.float32)
    first = 0.9 * moment_one + 0.1 * grad_f
    second = 0.95 * moment_two + 0.05 * grad_f * grad_f
    first_hat = first / (1.0 - jnp.power(jnp.float32(0.9), steps_f))
    second_hat = second / (1.0 - jnp.power(jnp.float32(0.95), steps_f))
    updated = master - 0.1 * (first_hat / (jnp.sqrt(second_hat) + 1e-08) + 0.1 * master)
    weight = token_mass(counts)
    states, mass = cycle_round([updated, first, second], weight, 0)
    states, unused = cycle_round(states, mass, 1)
    new_master, new_first, new_second = states
    rounded = new_master.astype(jnp.bfloat16)
    copies = jnp.broadcast_to(rounded[:, :, None], (N_ROW, N_COL, N_FSDP, ROWS, D))
    return (new_master, new_first, new_second, copies)
```

```python
import jax
import jax.numpy as jnp
from jax import lax
from jax.experimental import pallas as pl
from jax.experimental.pallas import tpu as pltpu
from jax.sharding import PartitionSpec as P

MESH = pl.DeviceIdType.MESH
X, M, V = 0, 1, 2
GROUPS = 3
CHUNKS = 9
D = 4096
HALF = D // 2
TILE = 512
SPAN = (14.0, 3.5, 3.5)
LEVELS = 32767.0


def wide(tile, columns):
    return jnp.concatenate([tile] * (columns // 128), axis=1)


def encode(value, span):
    size = jnp.maximum(jnp.abs(value) * (1.0 / span), 1e-30)
    root = lax.rsqrt(lax.rsqrt(size)) * LEVELS + 0.5
    level = jnp.minimum(root, LEVELS).astype(jnp.int32)
    return jnp.where(value < 0.0, -level, level)


def decode(code, span):
    root = code.astype(jnp.int32).astype(jnp.float32) * (1.0 / LEVELS)
    square = root * root
    return (square * span) * (root * jnp.abs(root))


def power(base, steps):
    result = jnp.full(steps.shape, 1.0, jnp.float32)
    for bit in range(11):
        factor = jnp.float32(base ** (2**bit))
        result = jnp.where((steps >> bit) & 1 == 1, result * factor, result)
    return jnp.where(steps >= 2048, 0.0, result)


SCHEDULE = (
    "A0", "A1", "B0", "A2", "A3", "B1", "A4", "B2", "A5", "A6",
    "B3", "C0", "A7", "B4", "C1", "A8", "B5", "C2", "B6", "B7",
    "B8", "G1", "G2", "C3", "G3", "C4", "G4", "C5", "G5", "C6",
    "G6", "C7", "G7", "C8",
)


def kernel(
    master, moment_one, moment_two, grads, counts, step,
    new_master, new_one, new_two, whole,
    grad_f, own, below, above, rowed, side, sent, got,
    tok, mass,
    row_send, row_recv, x_send, x_recv, z_send, z_recv, tok_send, tok_recv,
    ag_send, ag_recv,
):
    r, c, f = lax.axis_index("row"), lax.axis_index("col"), lax.axis_index("fsdp")
    nr, nc, nf = (lax.axis_size(a) for a in ("row", "col", "fsdp"))
    hi = lax.rem(c, 2)
    up, down = (lax.rem(r + 1, nr), c, f), (lax.rem(r + nr - 1, nr), c, f)
    plus, minus = lax.rem(c + 2, nc), lax.rem(c + nc - 2, nc)
    x_to = (r, hi * plus + (1 - hi) * minus, f)
    z_to = (r, c + 1 - 2 * hi, f)
    right, left = (r, c, lax.rem(f + 1, nf)), (r, c, lax.rem(f + nf - 1, nf))

    barrier = pltpu.get_barrier_semaphore()
    for other in (up, down, (r, plus, f), (r, minus, f), z_to, right, left):
        pl.semaphore_signal(barrier, 1, device_id=other, device_id_type=MESH)
    pl.semaphore_wait(barrier, 7)

    def remote(src, dst, send, recv, to):
        return pltpu.make_async_remote_copy(
            src_ref=src, dst_ref=dst, send_sem=send, recv_sem=recv, device_id=to, device_id_type=MESH
        )

    def tok_copy(i):
        src, dst, to = (
            (tok.at[0], tok.at[1], up),
            (tok.at[0], tok.at[2], down),
            (mass.at[0], mass.at[1], x_to),
            (mass.at[2], mass.at[3], z_to),
        )[i]
        return remote(src, dst, tok_send.at[i], tok_recv.at[i], to)

    def row_copy(i, q):
        dst, to = ((below, up), (above, down))[i]
        return remote(own.at[q], dst.at[q], row_send.at[i, q], row_recv.at[i, q], to)

    def x_copy(q):
        return remote(rowed.at[q], side.at[q], x_send.at[q], x_recv.at[q], x_to)

    def z_copy(q):
        return remote(sent.at[q], got.at[q], z_send.at[q], z_recv.at[q], z_to)

    def ag_copy(way, shard, g):
        at = shard * GROUPS + g
        return remote(whole.at[at], whole.at[at], ag_send.at[way, at], ag_recv.at[at], (right, left)[way])

    def each_tile(columns, body):
        def one(i, carry):
            body(pl.multiple_of(i * TILE, TILE))
            return carry

        lax.fori_loop(0, columns // TILE, one, 0)

    total = counts[0]
    for b in range(1, counts.shape[0]):
        total = total + counts[b] * (2**b)
    weight = jnp.full((8, 128), (total * 256).astype(jnp.float32), jnp.float32)
    tok[0] = weight
    tok_copy(0).start()
    tok_copy(1).start()

    def to_float(at):
        cols = pl.ds(at, TILE)
        grad_f[:, cols] = grads[:, cols].astype(jnp.float32)

    each_tile(D, to_float)

    steps = jnp.full((8, 128), step[0], jnp.int32)
    fix_one = wide(1.0 / (1.0 - power(0.9, steps)), TILE)
    fix_two = wide(1.0 / (1.0 - power(0.95, steps)), TILE)
    weight = wide(weight, TILE)
    for g in range(GROUPS):

        def adam(at, g=g):
            cols, rows = pl.ds(at, TILE), pl.ds(8 * g, 8)
            grad = grad_f[rows, cols]
            first = 0.9 * moment_one[rows, cols] + 0.1 * grad
            second = 0.95 * moment_two[rows, cols] + 0.05 * grad * grad
            old = master[rows, cols]
            move = (first * fix_one) / (jnp.sqrt(second * fix_two) + 1e-08)
            own[X * GROUPS + g, :, cols] = (old - 0.1 * (move + 0.1 * old)) * weight
            own[M * GROUPS + g, :, cols] = first * weight
            own[V * GROUPS + g, :, cols] = second * weight

        each_tile(D, adam)
        row_copy(0, g).start()
        row_copy(1, g).start()
    for q in range(GROUPS, CHUNKS):
        row_copy(0, q).start()
        row_copy(1, q).start()

    def stage_a(q):
        if q == 0:
            tok_copy(0).wait_recv()
            tok_copy(1).wait_recv()
            mass[0] = tok[0] + tok[1] + tok[2]
            tok_copy(2).start()
        row_copy(0, q).wait_recv()
        row_copy(1, q).wait_recv()

        def body(at):
            cols = pl.ds(at, TILE)
            rowed[q, :, cols] = own[q, :, cols] + below[q, :, cols] + above[q, :, cols]

        each_tile(D, body)
        x_copy(q).start()

    def stage_b(q):
        if q == 0:
            tok_copy(2).wait_recv()
            mass[2] = mass[0] + mass[1]
            tok_copy(3).start()
        x_copy(q).wait_recv()
        scale = wide(1.0 / mass[2], TILE)
        span = SPAN[q // GROUPS]

        def body(at):
            halves = []
            for start in (0, HALF):
                cols = pl.ds(pl.multiple_of(at + start, TILE), TILE)
                halves.append(encode((rowed[q, :, cols] + side[q, :, cols]) * scale, span))
            sent[q, :, pl.ds(at, TILE)] = jnp.concatenate(halves, axis=0).astype(jnp.int16)

        each_tile(HALF, body)
        z_copy(q).start()

    def stage_c(q):
        if q == 0:
            tok_copy(3).wait_recv()
        z_copy(q).wait_recv()
        back = wide(mass[3], TILE)
        scale = wide(1.0 / (mass[0] + mass[3]), TILE)
        state, g = divmod(q, GROUPS)
        out = (new_master, new_one, new_two)[state]

        def body(at):
            other = decode(got[q, :, pl.ds(at, TILE)], SPAN[state])
            halves = []
            for i, start in enumerate((0, HALF)):
                cols = pl.ds(pl.multiple_of(at + start, TILE), TILE)
                mean = (rowed[q, :, cols] + other[8 * i : 8 * i + 8] * back) * scale
                out[8 * g : 8 * g + 8, cols] = mean
                halves.append(mean)
            if state == X:
                whole[f * GROUPS + g, :, pl.ds(at, TILE)] = jnp.concatenate(halves, axis=0).astype(jnp.bfloat16)

        each_tile(HALF, body)
        if state == X:

            @pl.when(f < nf - 1)
            def _():
                ag_copy(0, f, g).start()

            @pl.when(f > 0)
            def _():
                ag_copy(1, f, g).start()

    def stage_g(k):
        for g in range(GROUPS):

            @pl.when(f >= k)
            def _():
                ag_copy(0, f - k, g).wait_recv()

                @pl.when(f < nf - 1)
                def _():
                    ag_copy(0, f - k, g).start()

            @pl.when(f + k < nf)
            def _():
                ag_copy(1, f + k, g).wait_recv()

                @pl.when(f > 0)
                def _():
                    ag_copy(1, f + k, g).start()

    for name in SCHEDULE:
        {"A": stage_a, "B": stage_b, "C": stage_c, "G": stage_g}[name[0]](int(name[1:]))

    for i in range(4):
        tok_copy(i).wait_send()
    for q in range(CHUNKS):
        row_copy(0, q).wait_send()
        row_copy(1, q).wait_send()
        x_copy(q).wait_send()
        z_copy(q).wait_send()
    for k in range(nf):
        for g in range(GROUPS):

            @pl.when((f >= k) & (f < nf - 1))
            def _():
                ag_copy(0, f - k, g).wait_send()

            @pl.when((f + k < nf) & (f > 0))
            def _():
                ag_copy(1, f + k, g).wait_send()


def per_device(master, moment_one, moment_two, grads, counts, step):
    nf = lax.axis_size("fsdp")
    rows = master.shape[2]
    vmem = pl.BlockSpec(memory_space=pltpu.VMEM)
    smem = pl.BlockSpec(memory_space=pltpu.SMEM)
    state = jax.ShapeDtypeStruct((rows, D), jnp.float32)
    wide_chunks = pltpu.VMEM((CHUNKS, 8, D), jnp.float32)
    short_chunks = pltpu.VMEM((CHUNKS, 16, HALF), jnp.int16)
    dma = pltpu.SemaphoreType.DMA
    results = pl.pallas_call(
        kernel,
        out_shape=(state, state, state, jax.ShapeDtypeStruct((nf * GROUPS, 16, HALF), jnp.bfloat16)),
        in_specs=[vmem] * 4 + [smem] * 2,
        out_specs=[vmem] * 4,
        scratch_shapes=[pltpu.VMEM((rows, D), jnp.float32)]
        + [wide_chunks] * 5
        + [short_chunks] * 2
        + [pltpu.VMEM((3, 8, 128), jnp.float32), pltpu.VMEM((4, 8, 128), jnp.float32)]
        + [dma((2, CHUNKS))] * 2
        + [dma((CHUNKS,))] * 4
        + [dma((4,))] * 2
        + [dma((2, nf * GROUPS)), dma((nf * GROUPS,))],
        compiler_params=pltpu.CompilerParams(
            collective_id=0, has_side_effects=True, vmem_limit_bytes=40 << 20
        ),
    )(
        *(a.reshape(rows, D) for a in (master, moment_one, moment_two, grads)),
        counts.reshape(counts.shape[-1]),
        step,
    )
    copies = results[3].reshape(nf * GROUPS, 2, 8, HALF).transpose(0, 2, 1, 3)
    return (
        *(a.reshape(1, 1, rows, D) for a in results[:3]),
        copies.reshape(1, 1, 1, nf * rows, D),
    )


def solution(mesh):
    split = P("row", "col", "fsdp", None)
    return jax.shard_map(
        per_device,
        mesh=mesh,
        in_specs=(split, split, split, split, P("row", "col", None), P()),
        out_specs=(split, split, split, P("row", "col", "fsdp", None, None)),
        check_vma=False,
    )
```

```python
import jax
import jax.numpy as jnp
from jax import lax
from jax.experimental import pallas as pl
from jax.experimental.pallas import tpu as pltpu
from jax.sharding import PartitionSpec as P

MESH = pl.DeviceIdType.MESH
X, M, V = 0, 1, 2
GROUPS = 3
CHUNKS = 9
D = 4096
HALF = D // 2
TILE = 512
SPAN = (14.0, 3.5, 3.5)
LEVELS = 32767.0


def wide(tile, columns):
    return jnp.concatenate([tile] * (columns // 128), axis=1)


def encode(value, span):
    size = jnp.maximum(jnp.abs(value) * (1.0 / span), 1e-30)
    root = lax.rsqrt(lax.rsqrt(size)) * LEVELS + 0.5
    level = jnp.minimum(root, LEVELS).astype(jnp.int32)
    return jnp.where(value < 0.0, -level, level)


def decode(code, span):
    root = code.astype(jnp.int32).astype(jnp.float32) * (1.0 / LEVELS)
    square = root * root
    return (square * span) * (root * jnp.abs(root))


def power(base, steps):
    result = jnp.full(steps.shape, 1.0, jnp.float32)
    for bit in range(11):
        factor = jnp.float32(base ** (2**bit))
        result = jnp.where((steps >> bit) & 1 == 1, result * factor, result)
    return jnp.where(steps >= 2048, 0.0, result)


SCHEDULE = (
    "A0", "A1", "B0", "A2", "A3", "B1", "A4", "B2", "A5", "A6",
    "B3", "C0", "A7", "B4", "C1", "A8", "B5", "C2", "B6", "B7",
    "B8", "G1", "G2", "C3", "G3", "C4", "G4", "C5", "G5", "C6",
    "G6", "C7", "G7", "C8",
)


def kernel(
    master, moment_one, moment_two, grads, counts, step,
    new_master, new_one, new_two, whole,
    grad_f, was, was_one, was_two, was_grad, own, below, above, rowed, side, sent, got,
    tok, mass, load,
    row_send, row_recv, x_send, x_recv, z_send, z_recv, tok_send, tok_recv,
    ag_send, ag_recv,
):
    r, c, f = lax.axis_index("row"), lax.axis_index("col"), lax.axis_index("fsdp")
    nr, nc, nf = (lax.axis_size(a) for a in ("row", "col", "fsdp"))
    hi = lax.rem(c, 2)
    up, down = (lax.rem(r + 1, nr), c, f), (lax.rem(r + nr - 1, nr), c, f)
    plus, minus = lax.rem(c + 2, nc), lax.rem(c + nc - 2, nc)
    x_to = (r, hi * plus + (1 - hi) * minus, f)
    z_to = (r, c + 1 - 2 * hi, f)
    right, left = (r, c, lax.rem(f + 1, nf)), (r, c, lax.rem(f + nf - 1, nf))

    barrier = pltpu.get_barrier_semaphore()
    for other in (up, down, (r, plus, f), (r, minus, f), z_to, right, left):
        pl.semaphore_signal(barrier, 1, device_id=other, device_id_type=MESH)

    loads = [pltpu.make_async_copy(grads, was_grad, load.at[0])]
    for g in range(GROUPS):
        rows = pl.ds(8 * g, 8)
        for i, (src, dst) in enumerate(((master, was), (moment_one, was_one), (moment_two, was_two))):
            loads.append(pltpu.make_async_copy(src.at[rows], dst.at[rows], load.at[1 + 3 * g + i]))
    for copy in loads:
        copy.start()

    def remote(src, dst, send, recv, to):
        return pltpu.make_async_remote_copy(
            src_ref=src, dst_ref=dst, send_sem=send, recv_sem=recv, device_id=to, device_id_type=MESH
        )

    def tok_copy(i):
        src, dst, to = (
            (tok.at[0], tok.at[1], up),
            (tok.at[0], tok.at[2], down),
            (mass.at[0], mass.at[1], x_to),
            (mass.at[2], mass.at[3], z_to),
        )[i]
        return remote(src, dst, tok_send.at[i], tok_recv.at[i], to)

    def row_copy(i, q):
        dst, to = ((below, up), (above, down))[i]
        return remote(own.at[q], dst.at[q], row_send.at[i, q], row_recv.at[i, q], to)

    def x_copy(q):
        return remote(rowed.at[q], side.at[q], x_send.at[q], x_recv.at[q], x_to)

    def z_copy(q):
        return remote(sent.at[q], got.at[q], z_send.at[q], z_recv.at[q], z_to)

    def ag_copy(way, shard, g):
        at = shard * GROUPS + g
        return remote(whole.at[at], whole.at[at], ag_send.at[way, at], ag_recv.at[at], (right, left)[way])

    def each_tile(columns, body):
        def one(i, carry):
            body(pl.multiple_of(i * TILE, TILE))
            return carry

        lax.fori_loop(0, columns // TILE, one, 0)

    total = counts[0]
    for b in range(1, counts.shape[0]):
        total = total + counts[b] * (2**b)
    weight = jnp.full((8, 128), (total * 256).astype(jnp.float32), jnp.float32)
    tok[0] = weight
    loads[0].wait()

    def to_float(at):
        cols = pl.ds(at, TILE)
        grad_f[:, cols] = was_grad[:, cols].astype(jnp.float32)

    each_tile(D, to_float)

    steps = jnp.full((8, 128), step[0], jnp.int32)
    fix_one = wide(1.0 / (1.0 - power(0.9, steps)), TILE)
    fix_two = wide(1.0 / (1.0 - power(0.95, steps)), TILE)
    weight = wide(weight, TILE)
    for g in range(GROUPS):
        for copy in loads[1 + 3 * g : 4 + 3 * g]:
            copy.wait()

        def adam(at, g=g):
            cols, rows = pl.ds(at, TILE), pl.ds(8 * g, 8)
            grad = grad_f[rows, cols]
            first = 0.9 * was_one[rows, cols] + 0.1 * grad
            second = 0.95 * was_two[rows, cols] + 0.05 * grad * grad
            old = was[rows, cols]
            move = (first * fix_one) / (jnp.sqrt(second * fix_two) + 1e-08)
            own[X * GROUPS + g, :, cols] = (old - 0.1 * (move + 0.1 * old)) * weight
            own[M * GROUPS + g, :, cols] = first * weight
            own[V * GROUPS + g, :, cols] = second * weight

        each_tile(D, adam)
        if g == 0:
            pl.semaphore_wait(barrier, 7)
            tok_copy(0).start()
            tok_copy(1).start()
        row_copy(0, g).start()
        row_copy(1, g).start()
    for q in range(GROUPS, CHUNKS):
        row_copy(0, q).start()
        row_copy(1, q).start()

    def stage_a(q):
        if q == 0:
            tok_copy(0).wait_recv()
            tok_copy(1).wait_recv()
            mass[0] = tok[0] + tok[1] + tok[2]
            tok_copy(2).start()
        row_copy(0, q).wait_recv()
        row_copy(1, q).wait_recv()

        def body(at):
            cols = pl.ds(at, TILE)
            rowed[q, :, cols] = own[q, :, cols] + below[q, :, cols] + above[q, :, cols]

        each_tile(D, body)
        x_copy(q).start()

    def stage_b(q):
        if q == 0:
            tok_copy(2).wait_recv()
            mass[2] = mass[0] + mass[1]
            tok_copy(3).start()
        x_copy(q).wait_recv()
        scale = wide(1.0 / mass[2], TILE)
        span = SPAN[q // GROUPS]

        def body(at):
            halves = []
            for start in (0, HALF):
                cols = pl.ds(pl.multiple_of(at + start, TILE), TILE)
                halves.append(encode((rowed[q, :, cols] + side[q, :, cols]) * scale, span))
            sent[q, :, pl.ds(at, TILE)] = jnp.concatenate(halves, axis=0).astype(jnp.int16)

        each_tile(HALF, body)
        z_copy(q).start()

    def stage_c(q):
        if q == 0:
            tok_copy(3).wait_recv()
        z_copy(q).wait_recv()
        back = wide(mass[3], TILE)
        scale = wide(1.0 / (mass[0] + mass[3]), TILE)
        state, g = divmod(q, GROUPS)
        out = (new_master, new_one, new_two)[state]

        def body(at):
            other = decode(got[q, :, pl.ds(at, TILE)], SPAN[state])
            halves = []
            for i, start in enumerate((0, HALF)):
                cols = pl.ds(pl.multiple_of(at + start, TILE), TILE)
                mean = (rowed[q, :, cols] + other[8 * i : 8 * i + 8] * back) * scale
                out[8 * g : 8 * g + 8, cols] = mean
                halves.append(mean)
            if state == X:
                whole[f * GROUPS + g, :, pl.ds(at, TILE)] = jnp.concatenate(halves, axis=0).astype(jnp.bfloat16)

        each_tile(HALF, body)
        if state == X:

            @pl.when(f < nf - 1)
            def _():
                ag_copy(0, f, g).start()

            @pl.when(f > 0)
            def _():
                ag_copy(1, f, g).start()

    def stage_g(k):
        for g in range(GROUPS):

            @pl.when(f >= k)
            def _():
                ag_copy(0, f - k, g).wait_recv()

                @pl.when(f < nf - 1)
                def _():
                    ag_copy(0, f - k, g).start()

            @pl.when(f + k < nf)
            def _():
                ag_copy(1, f + k, g).wait_recv()

                @pl.when(f > 0)
                def _():
                    ag_copy(1, f + k, g).start()

    for name in SCHEDULE:
        {"A": stage_a, "B": stage_b, "C": stage_c, "G": stage_g}[name[0]](int(name[1:]))

    for i in range(4):
        tok_copy(i).wait_send()
    for q in range(CHUNKS):
        row_copy(0, q).wait_send()
        row_copy(1, q).wait_send()
        x_copy(q).wait_send()
        z_copy(q).wait_send()
    for k in range(nf):
        for g in range(GROUPS):

            @pl.when((f >= k) & (f < nf - 1))
            def _():
                ag_copy(0, f - k, g).wait_send()

            @pl.when((f + k < nf) & (f > 0))
            def _():
                ag_copy(1, f + k, g).wait_send()


def place(*refs):
    copies = [pltpu.make_async_copy(refs[i], refs[4 + i], refs[8].at[i]) for i in range(4)]
    for copy in copies:
        copy.start()
    for copy in copies:
        copy.wait()


def per_device(master, moment_one, moment_two, grads, counts, step):
    nf = lax.axis_size("fsdp")
    rows = master.shape[2]
    vmem = pl.BlockSpec(memory_space=pltpu.VMEM)
    hbm = pl.BlockSpec(memory_space=pltpu.HBM)
    smem = pl.BlockSpec(memory_space=pltpu.SMEM)
    state = jax.ShapeDtypeStruct((rows, D), jnp.float32)
    wide_chunks = pltpu.VMEM((CHUNKS, 8, D), jnp.float32)
    short_chunks = pltpu.VMEM((CHUNKS, 16, HALF), jnp.int16)
    dma = pltpu.SemaphoreType.DMA
    results = pl.pallas_call(
        kernel,
        out_shape=(state, state, state, jax.ShapeDtypeStruct((nf * GROUPS, 16, HALF), jnp.bfloat16)),
        in_specs=[hbm] * 4 + [smem] * 2,
        out_specs=[vmem] * 4,
        scratch_shapes=[pltpu.VMEM((rows, D), jnp.float32)] * 4
        + [pltpu.VMEM((rows, D), jnp.bfloat16)]
        + [wide_chunks] * 5
        + [short_chunks] * 2
        + [pltpu.VMEM((3, 8, 128), jnp.float32), pltpu.VMEM((4, 8, 128), jnp.float32)]
        + [dma((10,))]
        + [dma((2, CHUNKS))] * 2
        + [dma((CHUNKS,))] * 4
        + [dma((4,))] * 2
        + [dma((2, nf * GROUPS)), dma((nf * GROUPS,))],
        compiler_params=pltpu.CompilerParams(
            collective_id=0, has_side_effects=True, vmem_limit_bytes=60 << 20
        ),
    )(
        *(a.reshape(rows, D) for a in (master, moment_one, moment_two, grads)),
        counts.reshape(counts.shape[-1]),
        step,
    )
    results = (*results[:3], results[3].reshape(nf * GROUPS, 2, 8, HALF).transpose(0, 2, 1, 3).reshape(nf * rows, D))
    results = pl.pallas_call(
        place,
        out_shape=[jax.ShapeDtypeStruct(a.shape, a.dtype) for a in results],
        in_specs=[vmem] * 4,
        out_specs=[hbm] * 4,
        scratch_shapes=[dma((4,))],
    )(*results)
    return (
        *(a.reshape(1, 1, rows, D) for a in results[:3]),
        results[3].reshape(1, 1, 1, nf * rows, D),
    )


def solution(mesh):
    split = P("row", "col", "fsdp", None)
    return jax.shard_map(
        per_device,
        mesh=mesh,
        in_specs=(split, split, split, split, P("row", "col", None), P()),
        out_specs=(split, split, split, P("row", "col", "fsdp", None, None)),
        check_vma=False,
    )
```

```python
import jax
import jax.numpy as jnp
from jax import lax
from jax.experimental import pallas as pl
from jax.experimental.pallas import tpu as pltpu
from jax.sharding import PartitionSpec as P

MESH = pl.DeviceIdType.MESH
X, M, V = 0, 1, 2
GROUPS = 3
CHUNKS = 9
D = 4096
HALF = D // 2
TILE = 512
SPAN = (14.0, 3.5, 3.5)
LEVELS = 32767.0


def wide(tile, columns):
    return jnp.concatenate([tile] * (columns // 128), axis=1)


def encode(value, span):
    size = jnp.maximum(jnp.abs(value) * (1.0 / span), 1e-30)
    root = lax.rsqrt(lax.rsqrt(size)) * LEVELS + 0.5
    level = jnp.minimum(root, LEVELS).astype(jnp.int32)
    return jnp.where(value < 0.0, -level, level)


def decode(code, span):
    root = code.astype(jnp.int32).astype(jnp.float32) * (1.0 / LEVELS)
    square = root * root
    return (square * span) * (root * jnp.abs(root))


def power(base, steps):
    result = jnp.full(steps.shape, 1.0, jnp.float32)
    for bit in range(11):
        factor = jnp.float32(base ** (2**bit))
        result = jnp.where((steps >> bit) & 1 == 1, result * factor, result)
    return jnp.where(steps >= 2048, 0.0, result)


SCHEDULE = (
    "Z3", "X0", "Z4", "R0", "X1", "Z5", "F0", "R1", "Z6", "X2",
    "F1", "R2", "Z7", "X3", "F2", "R3", "G1", "Z8", "X4", "F3",
    "R4", "G2", "X5", "F4", "R5", "G3", "X6", "F5", "R6", "G4",
    "X7", "F6", "R7", "G5", "X8", "F7", "R8", "G6", "G7", "F8",
)


def kernel(
    master, moment_one, moment_two, grads, counts, step,
    new_master, new_one, new_two, whole,
    grad_f, was, was_one, was_two, was_grad, own, summed, below, above, side, sent, got,
    tok, load,
    row_send, row_recv, x_send, x_recv, z_send, z_recv, tok_send, tok_recv,
    ag_send, ag_recv,
):
    r, c, f = lax.axis_index("row"), lax.axis_index("col"), lax.axis_index("fsdp")
    nr, nc, nf = (lax.axis_size(a) for a in ("row", "col", "fsdp"))
    hi = lax.rem(c, 2)
    up, down = (lax.rem(r + 1, nr), c, f), (lax.rem(r + nr - 1, nr), c, f)
    plus, minus = lax.rem(c + 2, nc), lax.rem(c + nc - 2, nc)
    x_to = (r, hi * minus + (1 - hi) * plus, f)
    z_to = (r, c + 1 - 2 * hi, f)
    right, left = (r, c, lax.rem(f + 1, nf)), (r, c, lax.rem(f + nf - 1, nf))

    barrier = pltpu.get_barrier_semaphore()
    for other in (up, down, (r, plus, f), (r, minus, f), z_to, right, left):
        pl.semaphore_signal(barrier, 1, device_id=other, device_id_type=MESH)

    loads = [pltpu.make_async_copy(grads, was_grad, load.at[0])]
    for g in range(GROUPS):
        rows = pl.ds(8 * g, 8)
        for i, (src, dst) in enumerate(((master, was), (moment_one, was_one), (moment_two, was_two))):
            loads.append(pltpu.make_async_copy(src.at[rows], dst.at[rows], load.at[1 + 3 * g + i]))
    for copy in loads:
        copy.start()

    def remote(src, dst, send, recv, to):
        return pltpu.make_async_remote_copy(
            src_ref=src, dst_ref=dst, send_sem=send, recv_sem=recv, device_id=to, device_id_type=MESH
        )

    def tok_copy(i):
        src, dst, to = ((0, 1, z_to), (1, 2, x_to), (3, 4, up), (3, 5, down))[i]
        return remote(tok.at[src], tok.at[dst], tok_send.at[i], tok_recv.at[i], to)

    def row_copy(i, q):
        dst, to = ((below, up), (above, down))[i]
        return remote(summed.at[q], dst.at[q], row_send.at[i, q], row_recv.at[i, q], to)

    def x_copy(q):
        return remote(got.at[q], side.at[q], x_send.at[q], x_recv.at[q], x_to)

    def z_copy(q):
        return remote(sent.at[q], got.at[q], z_send.at[q], z_recv.at[q], z_to)

    def ag_copy(way, shard, g):
        at = shard * GROUPS + g
        return remote(whole.at[at], whole.at[at], ag_send.at[way, at], ag_recv.at[at], (right, left)[way])

    def each_tile(columns, body):
        def one(i, carry):
            body(pl.multiple_of(i * TILE, TILE))
            return carry

        lax.fori_loop(0, columns // TILE, one, 0)

    total = counts[0]
    for b in range(1, counts.shape[0]):
        total = total + counts[b] * (2**b)
    weight = jnp.full((8, 128), (total * 256).astype(jnp.float32), jnp.float32)
    tok[0] = weight
    loads[0].wait()

    def to_float(at):
        cols = pl.ds(at, TILE)
        grad_f[:, cols] = was_grad[:, cols].astype(jnp.float32)

    each_tile(D, to_float)

    steps = jnp.full((8, 128), step[0], jnp.int32)
    fix_one = wide(1.0 / (1.0 - power(0.9, steps)), TILE)
    fix_two = wide(1.0 / (1.0 - power(0.95, steps)), TILE)

    def stage_z(q):
        span = SPAN[q // GROUPS]

        def body(at):
            halves = []
            for start in (0, HALF):
                cols = pl.ds(pl.multiple_of(at + start, TILE), TILE)
                halves.append(encode(own[q, :, cols], span))
            sent[q, :, pl.ds(at, TILE)] = jnp.concatenate(halves, axis=0).astype(jnp.int16)

        each_tile(HALF, body)
        if q == 0:
            pl.semaphore_wait(barrier, 7)
            tok_copy(0).start()
        z_copy(q).start()

    for g in range(GROUPS):
        for copy in loads[1 + 3 * g : 4 + 3 * g]:
            copy.wait()

        def adam(at, g=g):
            cols, rows = pl.ds(at, TILE), pl.ds(8 * g, 8)
            grad = grad_f[rows, cols]
            first = 0.9 * was_one[rows, cols] + 0.1 * grad
            second = 0.95 * was_two[rows, cols] + 0.05 * grad * grad
            old = was[rows, cols]
            move = (first * fix_one) / (jnp.sqrt(second * fix_two) + 1e-08)
            own[X * GROUPS + g, :, cols] = old - 0.1 * (move + 0.1 * old)
            own[M * GROUPS + g, :, cols] = first
            own[V * GROUPS + g, :, cols] = second

        each_tile(D, adam)
        stage_z(g)

    def stage_x(q):
        if q == 0:
            tok_copy(0).wait_recv()
            tok_copy(1).start()
        z_copy(q).wait_recv()
        x_copy(q).start()

    def stage_r(q):
        if q == 0:
            tok_copy(1).wait_recv()
            tok[3] = tok[0] + tok[1] + tok[2]
            tok_copy(2).start()
            tok_copy(3).start()
        x_copy(q).wait_recv()
        here, facing, beyond = (wide(tok[i], TILE) for i in range(3))
        span = SPAN[q // GROUPS]

        def body(at):
            one = decode(got[q, :, pl.ds(at, TILE)], span)
            two = decode(side[q, :, pl.ds(at, TILE)], span)
            for i, start in ((0, 0), (8, HALF)):
                cols = pl.ds(pl.multiple_of(at + start, TILE), TILE)
                summed[q, :, cols] = own[q, :, cols] * here + one[i : i + 8] * facing + two[i : i + 8] * beyond

        each_tile(HALF, body)
        row_copy(0, q).start()
        row_copy(1, q).start()

    def stage_f(q):
        if q == 0:
            tok_copy(2).wait_recv()
            tok_copy(3).wait_recv()
        row_copy(0, q).wait_recv()
        row_copy(1, q).wait_recv()
        scale = wide(1.0 / (tok[3] + tok[4] + tok[5]), TILE)
        state, g = divmod(q, GROUPS)
        out = (new_master, new_one, new_two)[state]

        def body(at):
            halves = []
            for start in (0, HALF):
                cols = pl.ds(pl.multiple_of(at + start, TILE), TILE)
                mean = (summed[q, :, cols] + below[q, :, cols] + above[q, :, cols]) * scale
                out[8 * g : 8 * g + 8, cols] = mean
                halves.append(mean)
            if state == X:
                whole[f * GROUPS + g, :, pl.ds(at, TILE)] = jnp.concatenate(halves, axis=0).astype(jnp.bfloat16)

        each_tile(HALF, body)
        if state == X:

            @pl.when(f < nf - 1)
            def _():
                ag_copy(0, f, g).start()

            @pl.when(f > 0)
            def _():
                ag_copy(1, f, g).start()

    def stage_g(k):
        for g in range(GROUPS):

            @pl.when(f >= k)
            def _():
                ag_copy(0, f - k, g).wait_recv()

                @pl.when(f < nf - 1)
                def _():
                    ag_copy(0, f - k, g).start()

            @pl.when(f + k < nf)
            def _():
                ag_copy(1, f + k, g).wait_recv()

                @pl.when(f > 0)
                def _():
                    ag_copy(1, f + k, g).start()

    stages = dict(Z=stage_z, X=stage_x, R=stage_r, F=stage_f, G=stage_g)
    for name in SCHEDULE:
        stages[name[0]](int(name[1:]))

    for i in range(4):
        tok_copy(i).wait_send()
    for q in range(CHUNKS):
        row_copy(0, q).wait_send()
        row_copy(1, q).wait_send()
        x_copy(q).wait_send()
        z_copy(q).wait_send()
    for k in range(nf):
        for g in range(GROUPS):

            @pl.when((f >= k) & (f < nf - 1))
            def _():
                ag_copy(0, f - k, g).wait_send()

            @pl.when((f + k < nf) & (f > 0))
            def _():
                ag_copy(1, f + k, g).wait_send()


def place(*refs):
    copies = [pltpu.make_async_copy(refs[i], refs[4 + i], refs[8].at[i]) for i in range(4)]
    for copy in copies:
        copy.start()
    for copy in copies:
        copy.wait()


def per_device(master, moment_one, moment_two, grads, counts, step):
    nf = lax.axis_size("fsdp")
    rows = master.shape[2]
    vmem = pl.BlockSpec(memory_space=pltpu.VMEM)
    hbm = pl.BlockSpec(memory_space=pltpu.HBM)
    smem = pl.BlockSpec(memory_space=pltpu.SMEM)
    state = jax.ShapeDtypeStruct((rows, D), jnp.float32)
    wide_chunks = pltpu.VMEM((CHUNKS, 8, D), jnp.float32)
    short_chunks = pltpu.VMEM((CHUNKS, 16, HALF), jnp.int16)
    dma = pltpu.SemaphoreType.DMA
    results = pl.pallas_call(
        kernel,
        out_shape=(state, state, state, jax.ShapeDtypeStruct((nf * GROUPS, 16, HALF), jnp.bfloat16)),
        in_specs=[hbm] * 4 + [smem] * 2,
        out_specs=[vmem] * 4,
        scratch_shapes=[pltpu.VMEM((rows, D), jnp.float32)] * 4
        + [pltpu.VMEM((rows, D), jnp.bfloat16)]
        + [wide_chunks] * 4
        + [short_chunks] * 3
        + [pltpu.VMEM((6, 8, 128), jnp.float32)]
        + [dma((10,))]
        + [dma((2, CHUNKS))] * 2
        + [dma((CHUNKS,))] * 4
        + [dma((4,))] * 2
        + [dma((2, nf * GROUPS)), dma((nf * GROUPS,))],
        compiler_params=pltpu.CompilerParams(
            collective_id=0, has_side_effects=True, vmem_limit_bytes=60 << 20
        ),
    )(
        *(a.reshape(rows, D) for a in (master, moment_one, moment_two, grads)),
        counts.reshape(counts.shape[-1]),
        step,
    )
    results = (*results[:3], results[3].reshape(nf * GROUPS, 2, 8, HALF).transpose(0, 2, 1, 3).reshape(nf * rows, D))
    results = pl.pallas_call(
        place,
        out_shape=[jax.ShapeDtypeStruct(a.shape, a.dtype) for a in results],
        in_specs=[vmem] * 4,
        out_specs=[hbm] * 4,
        scratch_shapes=[dma((4,))],
    )(*results)
    return (
        *(a.reshape(1, 1, rows, D) for a in results[:3]),
        results[3].reshape(1, 1, 1, nf * rows, D),
    )


def solution(mesh):
    split = P("row", "col", "fsdp", None)
    return jax.shard_map(
        per_device,
        mesh=mesh,
        in_specs=(split, split, split, split, P("row", "col", None), P()),
        out_specs=(split, split, split, P("row", "col", "fsdp", None, None)),
        check_vma=False,
    )
```

```python
import jax
import jax.numpy as jnp
from jax import lax
from jax.experimental import pallas as pl
from jax.experimental.pallas import tpu as pltpu
from jax.sharding import PartitionSpec as P

MESH = pl.DeviceIdType.MESH
X, M, V = 0, 1, 2
GROUPS = 3
CHUNKS = 9
D = 4096
HALF = D // 2
TILE = 512
SPAN = (14.0, 3.5, 3.5)
LEVELS = 32767.0


def wide(tile, columns):
    return jnp.concatenate([tile] * (columns // 128), axis=1)


def encode(value, span):
    size = jnp.maximum(jnp.abs(value) * (1.0 / span), 1e-30)
    root = lax.rsqrt(lax.rsqrt(size)) * LEVELS + 0.5
    level = jnp.minimum(root, LEVELS).astype(jnp.int32)
    return jnp.where(value < 0.0, -level, level)


def decode(code, span):
    root = code.astype(jnp.int32).astype(jnp.float32) * (1.0 / LEVELS)
    square = root * root
    return (square * span) * (root * jnp.abs(root))


def power(base, steps):
    result = jnp.full(steps.shape, 1.0, jnp.float32)
    for bit in range(11):
        factor = jnp.float32(base ** (2**bit))
        result = jnp.where((steps >> bit) & 1 == 1, result * factor, result)
    return jnp.where(steps >= 2048, 0.0, result)


SCHEDULE = (
    "Z3", "X0", "Z4", "R0", "X1", "Z5", "F0", "R1", "X2", "Z6",
    "F1", "R2", "Z7", "F2", "X3", "Z8", "R3", "X4", "F3", "R4",
    "X5", "G1", "F4", "R5", "X6", "G2", "F5", "R6", "X7", "G3",
    "F6", "R7", "X8", "G4", "F7", "R8", "G5", "F8", "G6", "G7",
)


def kernel(
    master, moment_one, moment_two, grads, counts, step,
    out_master, out_one, out_two, out_whole,
    new_master, new_one, new_two, whole, out_send, whole_send,
    grad_f, was, was_one, was_two, was_grad, own, summed, below, above, side, sent, got,
    tok, load,
    row_send, row_recv, x_send, x_recv, z_send, z_recv, tok_send, tok_recv,
    ag_send, ag_recv,
):
    r, c, f = lax.axis_index("row"), lax.axis_index("col"), lax.axis_index("fsdp")
    nr, nc, nf = (lax.axis_size(a) for a in ("row", "col", "fsdp"))
    hi = lax.rem(c, 2)
    up, down = (lax.rem(r + 1, nr), c, f), (lax.rem(r + nr - 1, nr), c, f)
    plus, minus = lax.rem(c + 2, nc), lax.rem(c + nc - 2, nc)
    x_to = (r, hi * minus + (1 - hi) * plus, f)
    z_to = (r, c + 1 - 2 * hi, f)
    right, left = (r, c, lax.rem(f + 1, nf)), (r, c, lax.rem(f + nf - 1, nf))

    barrier = pltpu.get_barrier_semaphore()
    for other in (up, down, (r, plus, f), (r, minus, f), z_to, right, left):
        pl.semaphore_signal(barrier, 1, device_id=other, device_id_type=MESH)

    loads = [pltpu.make_async_copy(grads, was_grad, load.at[0])]
    for g in range(GROUPS):
        rows = pl.ds(8 * g, 8)
        for i, (src, dst) in enumerate(((master, was), (moment_one, was_one), (moment_two, was_two))):
            loads.append(pltpu.make_async_copy(src.at[rows], dst.at[rows], load.at[1 + 3 * g + i]))
    for copy in loads:
        copy.start()

    def remote(src, dst, send, recv, to):
        return pltpu.make_async_remote_copy(
            src_ref=src, dst_ref=dst, send_sem=send, recv_sem=recv, device_id=to, device_id_type=MESH
        )

    def tok_copy(i):
        src, dst, to = ((0, 1, z_to), (1, 2, x_to), (3, 4, up), (3, 5, down))[i]
        return remote(tok.at[src], tok.at[dst], tok_send.at[i], tok_recv.at[i], to)

    def row_copy(i, q):
        dst, to = ((below, up), (above, down))[i]
        return remote(summed.at[q], dst.at[q], row_send.at[i, q], row_recv.at[i, q], to)

    def x_copy(q):
        return remote(got.at[q], side.at[q], x_send.at[q], x_recv.at[q], x_to)

    def z_copy(q):
        return remote(sent.at[q], got.at[q], z_send.at[q], z_recv.at[q], z_to)

    def ag_copy(way, shard, g):
        at = shard * GROUPS + g
        return remote(whole.at[at], whole.at[at], ag_send.at[way, at], ag_recv.at[at], (right, left)[way])

    def out_copy(q):
        state, g = divmod(q, GROUPS)
        rows = pl.ds(8 * g, 8)
        src, dst = ((new_master, out_master), (new_one, out_one), (new_two, out_two))[state]
        return pltpu.make_async_copy(src.at[rows], dst.at[rows], out_send.at[q])

    def whole_copy(shard, g):
        at = shard * GROUPS + g
        return pltpu.make_async_copy(whole.at[at], out_whole.at[at], whole_send.at[at])

    def each_tile(columns, body):
        def one(i, carry):
            body(pl.multiple_of(i * TILE, TILE))
            return carry

        lax.fori_loop(0, columns // TILE, one, 0)

    total = counts[0]
    for b in range(1, counts.shape[0]):
        total = total + counts[b] * (2**b)
    weight = jnp.full((8, 128), (total * 256).astype(jnp.float32), jnp.float32)
    tok[0] = weight
    loads[0].wait()

    def to_float(at):
        cols = pl.ds(at, TILE)
        grad_f[:, cols] = was_grad[:, cols].astype(jnp.float32)

    each_tile(D, to_float)

    steps = jnp.full((8, 128), step[0], jnp.int32)
    fix_one = wide(1.0 / (1.0 - power(0.9, steps)), TILE)
    fix_two = wide(1.0 / (1.0 - power(0.95, steps)), TILE)

    def stage_z(q):
        span = SPAN[q // GROUPS]

        def body(at):
            halves = []
            for start in (0, HALF):
                cols = pl.ds(pl.multiple_of(at + start, TILE), TILE)
                halves.append(encode(own[q, :, cols], span))
            sent[q, :, pl.ds(at, TILE)] = jnp.concatenate(halves, axis=0).astype(jnp.int16)

        each_tile(HALF, body)
        if q == 0:
            pl.semaphore_wait(barrier, 7)
            tok_copy(0).start()
        z_copy(q).start()

    for g in range(GROUPS):
        for copy in loads[1 + 3 * g : 4 + 3 * g]:
            copy.wait()

        def adam(at, g=g):
            cols, rows = pl.ds(at, TILE), pl.ds(8 * g, 8)
            grad = grad_f[rows, cols]
            first = 0.9 * was_one[rows, cols] + 0.1 * grad
            second = 0.95 * was_two[rows, cols] + 0.05 * grad * grad
            old = was[rows, cols]
            move = (first * fix_one) / (jnp.sqrt(second * fix_two) + 1e-08)
            own[X * GROUPS + g, :, cols] = old - 0.1 * (move + 0.1 * old)
            own[M * GROUPS + g, :, cols] = first
            own[V * GROUPS + g, :, cols] = second

        each_tile(D, adam)
        stage_z(g)

    def stage_x(q):
        if q == 0:
            tok_copy(0).wait_recv()
            tok_copy(1).start()
        z_copy(q).wait_recv()
        x_copy(q).start()

    def stage_r(q):
        if q == 0:
            tok_copy(1).wait_recv()
            tok[3] = tok[0] + tok[1] + tok[2]
            tok_copy(2).start()
            tok_copy(3).start()
        x_copy(q).wait_recv()
        here, facing, beyond = (wide(tok[i], TILE) for i in range(3))
        span = SPAN[q // GROUPS]

        def body(at):
            one = decode(got[q, :, pl.ds(at, TILE)], span)
            two = decode(side[q, :, pl.ds(at, TILE)], span)
            for i, start in ((0, 0), (8, HALF)):
                cols = pl.ds(pl.multiple_of(at + start, TILE), TILE)
                summed[q, :, cols] = own[q, :, cols] * here + one[i : i + 8] * facing + two[i : i + 8] * beyond

        each_tile(HALF, body)
        row_copy(0, q).start()
        row_copy(1, q).start()

    def stage_f(q):
        if q == 0:
            tok_copy(2).wait_recv()
            tok_copy(3).wait_recv()
        row_copy(0, q).wait_recv()
        row_copy(1, q).wait_recv()
        scale = wide(1.0 / (tok[3] + tok[4] + tok[5]), TILE)
        state, g = divmod(q, GROUPS)
        out = (new_master, new_one, new_two)[state]

        def body(at):
            halves = []
            for start in (0, HALF):
                cols = pl.ds(pl.multiple_of(at + start, TILE), TILE)
                mean = (summed[q, :, cols] + below[q, :, cols] + above[q, :, cols]) * scale
                out[8 * g : 8 * g + 8, cols] = mean
                halves.append(mean)
            if state == X:
                whole[f * GROUPS + g, :, pl.ds(at, TILE)] = jnp.concatenate(halves, axis=0).astype(jnp.bfloat16)

        each_tile(HALF, body)
        out_copy(q).start()
        if state == X:
            whole_copy(f, g).start()

            @pl.when(f < nf - 1)
            def _():
                ag_copy(0, f, g).start()

            @pl.when(f > 0)
            def _():
                ag_copy(1, f, g).start()

    def stage_g(k):
        for g in range(GROUPS):

            @pl.when(f >= k)
            def _():
                ag_copy(0, f - k, g).wait_recv()
                whole_copy(f - k, g).start()

                @pl.when(f < nf - 1)
                def _():
                    ag_copy(0, f - k, g).start()

            @pl.when(f + k < nf)
            def _():
                ag_copy(1, f + k, g).wait_recv()
                whole_copy(f + k, g).start()

                @pl.when(f > 0)
                def _():
                    ag_copy(1, f + k, g).start()

    stages = dict(Z=stage_z, X=stage_x, R=stage_r, F=stage_f, G=stage_g)
    for name in SCHEDULE:
        stages[name[0]](int(name[1:]))

    for q in range(CHUNKS):
        out_copy(q).wait()
    for shard in range(nf):
        for g in range(GROUPS):
            whole_copy(shard, g).wait()
    for i in range(4):
        tok_copy(i).wait_send()
    for q in range(CHUNKS):
        row_copy(0, q).wait_send()
        row_copy(1, q).wait_send()
        x_copy(q).wait_send()
        z_copy(q).wait_send()
    for k in range(nf):
        for g in range(GROUPS):

            @pl.when((f >= k) & (f < nf - 1))
            def _():
                ag_copy(0, f - k, g).wait_send()

            @pl.when((f + k < nf) & (f > 0))
            def _():
                ag_copy(1, f + k, g).wait_send()


def place(*refs):
    sources, targets, held, (come, go) = refs[:4], refs[4:8], refs[8:12], refs[12:]
    pieces = [(i, 0, ref.shape[0]) for i, ref in enumerate(sources[:3])]
    rows = sources[3].shape[0] // 4
    pieces += [(3, rows * k, rows) for k in range(4)]
    loads, stores = [], []
    for n, (i, first, count) in enumerate(pieces):
        rows = pl.ds(first, count)
        loads.append(pltpu.make_async_copy(sources[i].at[rows], held[i].at[rows], come.at[n]))
        stores.append(pltpu.make_async_copy(held[i].at[rows], targets[i].at[rows], go.at[n]))
    for copy in loads:
        copy.start()
    for load, store in zip(loads, stores):
        load.wait()
        store.start()
    for copy in stores:
        copy.wait()


def per_device(master, moment_one, moment_two, grads, counts, step):
    nf = lax.axis_size("fsdp")
    rows = master.shape[2]
    vmem = pl.BlockSpec(memory_space=pltpu.VMEM)
    hbm = pl.BlockSpec(memory_space=pltpu.HBM)
    smem = pl.BlockSpec(memory_space=pltpu.SMEM)
    state = jax.ShapeDtypeStruct((rows, D), jnp.float32)
    wide_chunks = pltpu.VMEM((CHUNKS, 8, D), jnp.float32)
    short_chunks = pltpu.VMEM((CHUNKS, 16, HALF), jnp.int16)
    dma = pltpu.SemaphoreType.DMA
    results = pl.pallas_call(
        kernel,
        out_shape=(state, state, state, jax.ShapeDtypeStruct((nf * GROUPS, 16, HALF), jnp.bfloat16)),
        in_specs=[hbm] * 4 + [smem] * 2,
        out_specs=[hbm] * 4,
        scratch_shapes=[pltpu.VMEM((rows, D), jnp.float32)] * 3
        + [pltpu.VMEM((nf * GROUPS, 16, HALF), jnp.bfloat16), dma((CHUNKS,)), dma((nf * GROUPS,))]
        + [pltpu.VMEM((rows, D), jnp.float32)] * 4
        + [pltpu.VMEM((rows, D), jnp.bfloat16)]
        + [wide_chunks] * 4
        + [short_chunks] * 3
        + [pltpu.VMEM((6, 8, 128), jnp.float32)]
        + [dma((10,))]
        + [dma((2, CHUNKS))] * 2
        + [dma((CHUNKS,))] * 4
        + [dma((4,))] * 2
        + [dma((2, nf * GROUPS)), dma((nf * GROUPS,))],
        compiler_params=pltpu.CompilerParams(
            collective_id=0, has_side_effects=True, vmem_limit_bytes=60 << 20
        ),
    )(
        *(a.reshape(rows, D) for a in (master, moment_one, moment_two, grads)),
        counts.reshape(counts.shape[-1]),
        step,
    )
    results = (*results[:3], results[3].reshape(nf * GROUPS, 2, 8, HALF).transpose(0, 2, 1, 3).reshape(nf * rows, D))
    results = pl.pallas_call(
        place,
        out_shape=[jax.ShapeDtypeStruct(a.shape, a.dtype) for a in results],
        in_specs=[hbm] * 4,
        out_specs=[hbm] * 4,
        scratch_shapes=[pltpu.VMEM(a.shape, a.dtype) for a in results] + [dma((7,))] * 2,
        compiler_params=pltpu.CompilerParams(vmem_limit_bytes=60 << 20),
    )(*results)
    return (
        *(a.reshape(1, 1, rows, D) for a in results[:3]),
        results[3].reshape(1, 1, 1, nf * rows, D),
    )


def solution(mesh):
    split = P("row", "col", "fsdp", None)
    return jax.shard_map(
        per_device,
        mesh=mesh,
        in_specs=(split, split, split, split, P("row", "col", None), P()),
        out_specs=(split, split, split, P("row", "col", "fsdp", None, None)),
        check_vma=False,
    )
```

```python
import jax
import jax.numpy as jnp
from jax import lax
from jax.experimental import pallas as pl
from jax.experimental.pallas import tpu as pltpu
from jax.sharding import PartitionSpec as P

MESH = pl.DeviceIdType.MESH
X, M, V = 0, 1, 2
GROUPS = 3
CHUNKS = 9
D = 4096
HALF = D // 2
TILE = 512
SPAN = (14.0, 3.5, 3.5)
LEVELS = 32767.0


def wide(tile, columns):
    return jnp.concatenate([tile] * (columns // 128), axis=1)


def encode(value, span):
    size = jnp.maximum(jnp.abs(value) * (1.0 / span), 1e-30)
    root = lax.rsqrt(lax.rsqrt(size)) * LEVELS + 0.5
    level = jnp.minimum(root, LEVELS).astype(jnp.int32)
    return jnp.where(value < 0.0, -level, level)


def decode(code, span):
    root = code.astype(jnp.int32).astype(jnp.float32) * (1.0 / LEVELS)
    square = root * root
    return (square * span) * (root * jnp.abs(root))


def power(base, steps):
    result = jnp.full(steps.shape, 1.0, jnp.float32)
    for bit in range(11):
        factor = jnp.float32(base ** (2**bit))
        result = jnp.where((steps >> bit) & 1 == 1, result * factor, result)
    return jnp.where(steps >= 2048, 0.0, result)


SCHEDULE = (
    "Z3", "X0", "Z4", "R0", "X1", "F0", "Z5", "R1", "X2", "Z6",
    "F1", "Z7", "R2", "F2", "X3", "Z8", "R3", "X4", "F3", "R4",
    "X5", "G1", "F4", "R5", "X6", "G2", "G3", "F5", "R6", "X7",
    "G4", "F6", "R7", "X8", "G5", "F7", "R8", "G6", "F8", "G7",
)


def kernel(
    master, moment_one, moment_two, grads, counts, step,
    out_master, out_one, out_two, out_whole,
    new_master, new_one, new_two, whole, out_send, whole_send,
    grad_f, was, was_one, was_two, was_grad, own, summed, below, above, side, sent, got,
    tok, load,
    row_send, row_recv, x_send, x_recv, z_send, z_recv, tok_send, tok_recv,
    ag_send, ag_recv,
):
    r, c, f = lax.axis_index("row"), lax.axis_index("col"), lax.axis_index("fsdp")
    nr, nc, nf = (lax.axis_size(a) for a in ("row", "col", "fsdp"))
    hi = lax.rem(c, 2)
    up, down = (lax.rem(r + 1, nr), c, f), (lax.rem(r + nr - 1, nr), c, f)
    plus, minus = lax.rem(c + 2, nc), lax.rem(c + nc - 2, nc)
    x_to = (r, hi * minus + (1 - hi) * plus, f)
    z_to = (r, c + 1 - 2 * hi, f)
    right, left = (r, c, lax.rem(f + 1, nf)), (r, c, lax.rem(f + nf - 1, nf))

    barrier = pltpu.get_barrier_semaphore()
    for other in (up, down, (r, plus, f), (r, minus, f), z_to, right, left):
        pl.semaphore_signal(barrier, 1, device_id=other, device_id_type=MESH)

    loads = [pltpu.make_async_copy(grads, was_grad, load.at[0])]
    for g in range(GROUPS):
        rows = pl.ds(8 * g, 8)
        for i, (src, dst) in enumerate(((master, was), (moment_one, was_one), (moment_two, was_two))):
            loads.append(pltpu.make_async_copy(src.at[rows], dst.at[rows], load.at[1 + 3 * g + i]))
    for copy in loads:
        copy.start()

    def remote(src, dst, send, recv, to):
        return pltpu.make_async_remote_copy(
            src_ref=src, dst_ref=dst, send_sem=send, recv_sem=recv, device_id=to, device_id_type=MESH
        )

    def tok_copy(i):
        src, dst, to = ((0, 1, z_to), (1, 2, x_to), (3, 4, up), (3, 5, down))[i]
        return remote(tok.at[src], tok.at[dst], tok_send.at[i], tok_recv.at[i], to)

    def row_copy(i, q):
        dst, to = ((below, up), (above, down))[i]
        return remote(summed.at[q], dst.at[q], row_send.at[i, q], row_recv.at[i, q], to)

    def x_copy(q):
        return remote(got.at[q], side.at[q], x_send.at[q], x_recv.at[q], x_to)

    def z_copy(q):
        return remote(sent.at[q], got.at[q], z_send.at[q], z_recv.at[q], z_to)

    def ag_copy(way, shard, g):
        at = shard * GROUPS + g
        return remote(whole.at[at], whole.at[at], ag_send.at[way, at], ag_recv.at[at], (right, left)[way])

    def out_copy(q):
        state, g = divmod(q, GROUPS)
        rows = pl.ds(8 * g, 8)
        src, dst = ((new_master, out_master), (new_one, out_one), (new_two, out_two))[state]
        return pltpu.make_async_copy(src.at[rows], dst.at[rows], out_send.at[q])

    def whole_copy(shard, g):
        at = shard * GROUPS + g
        return pltpu.make_async_copy(whole.at[at], out_whole.at[at], whole_send.at[at])

    def each_tile(columns, body):
        def one(i, carry):
            body(pl.multiple_of(i * TILE, TILE))
            return carry

        lax.fori_loop(0, columns // TILE, one, 0)

    total = counts[0]
    for b in range(1, counts.shape[0]):
        total = total + counts[b] * (2**b)
    weight = jnp.full((8, 128), (total * 256).astype(jnp.float32), jnp.float32)
    tok[0] = weight
    loads[0].wait()

    def to_float(at):
        cols = pl.ds(at, TILE)
        grad_f[:, cols] = was_grad[:, cols].astype(jnp.float32)

    each_tile(D, to_float)

    steps = jnp.full((8, 128), step[0], jnp.int32)
    fix_one = wide(1.0 / (1.0 - power(0.9, steps)), TILE)
    fix_two = wide(1.0 / (1.0 - power(0.95, steps)), TILE)

    def stage_z(q):
        span = SPAN[q // GROUPS]

        def body(at):
            halves = []
            for start in (0, HALF):
                cols = pl.ds(pl.multiple_of(at + start, TILE), TILE)
                halves.append(encode(own[q, :, cols], span))
            sent[q, :, pl.ds(at, TILE)] = jnp.concatenate(halves, axis=0).astype(jnp.int16)

        each_tile(HALF, body)
        if q == 0:
            pl.semaphore_wait(barrier, 7)
            tok_copy(0).start()
        z_copy(q).start()

    for g in range(GROUPS):
        for copy in loads[1 + 3 * g : 4 + 3 * g]:
            copy.wait()

        def adam(at, g=g):
            cols, rows = pl.ds(at, TILE), pl.ds(8 * g, 8)
            grad = grad_f[rows, cols]
            first = 0.9 * was_one[rows, cols] + 0.1 * grad
            second = 0.95 * was_two[rows, cols] + 0.05 * grad * grad
            old = was[rows, cols]
            move = (first * fix_one) / (jnp.sqrt(second * fix_two) + 1e-08)
            own[X * GROUPS + g, :, cols] = old - 0.1 * (move + 0.1 * old)
            own[M * GROUPS + g, :, cols] = first
            own[V * GROUPS + g, :, cols] = second

        each_tile(D, adam)
        stage_z(g)

    def stage_x(q):
        if q == 0:
            tok_copy(0).wait_recv()
            tok_copy(1).start()
        z_copy(q).wait_recv()
        x_copy(q).start()

    def stage_r(q):
        if q == 0:
            tok_copy(1).wait_recv()
            tok[3] = tok[0] + tok[1] + tok[2]
            tok_copy(2).start()
            tok_copy(3).start()
        x_copy(q).wait_recv()
        here, facing, beyond = (wide(tok[i], TILE) for i in range(3))
        span = SPAN[q // GROUPS]

        def body(at):
            one = decode(got[q, :, pl.ds(at, TILE)], span)
            two = decode(side[q, :, pl.ds(at, TILE)], span)
            for i, start in ((0, 0), (8, HALF)):
                cols = pl.ds(pl.multiple_of(at + start, TILE), TILE)
                summed[q, :, cols] = own[q, :, cols] * here + one[i : i + 8] * facing + two[i : i + 8] * beyond

        each_tile(HALF, body)
        row_copy(0, q).start()
        row_copy(1, q).start()

    def stage_f(q):
        if q == 0:
            tok_copy(2).wait_recv()
            tok_copy(3).wait_recv()
        row_copy(0, q).wait_recv()
        row_copy(1, q).wait_recv()
        scale = wide(1.0 / (tok[3] + tok[4] + tok[5]), TILE)
        state, g = divmod(q, GROUPS)
        out = (new_master, new_one, new_two)[state]

        def body(at):
            halves = []
            for start in (0, HALF):
                cols = pl.ds(pl.multiple_of(at + start, TILE), TILE)
                mean = (summed[q, :, cols] + below[q, :, cols] + above[q, :, cols]) * scale
                out[8 * g : 8 * g + 8, cols] = mean
                halves.append(mean)
            if state == X:
                whole[f * GROUPS + g, :, pl.ds(at, TILE)] = jnp.concatenate(halves, axis=0).astype(jnp.bfloat16)

        each_tile(HALF, body)
        out_copy(q).start()
        if state == X:
            whole_copy(f, g).start()

            @pl.when(f < nf - 1)
            def _():
                ag_copy(0, f, g).start()

            @pl.when(f > 0)
            def _():
                ag_copy(1, f, g).start()

    def stage_g(k):
        for g in range(GROUPS):

            @pl.when(f >= k)
            def _():
                ag_copy(0, f - k, g).wait_recv()
                whole_copy(f - k, g).start()

                @pl.when(f < nf - 1)
                def _():
                    ag_copy(0, f - k, g).start()

            @pl.when(f + k < nf)
            def _():
                ag_copy(1, f + k, g).wait_recv()
                whole_copy(f + k, g).start()

                @pl.when(f > 0)
                def _():
                    ag_copy(1, f + k, g).start()

    stages = dict(Z=stage_z, X=stage_x, R=stage_r, F=stage_f, G=stage_g)
    for name in SCHEDULE:
        stages[name[0]](int(name[1:]))

    for q in range(CHUNKS):
        out_copy(q).wait()
    for shard in range(nf):
        for g in range(GROUPS):
            whole_copy(shard, g).wait()
    for i in range(4):
        tok_copy(i).wait_send()
    for q in range(CHUNKS):
        row_copy(0, q).wait_send()
        row_copy(1, q).wait_send()
        x_copy(q).wait_send()
        z_copy(q).wait_send()
    for k in range(nf):
        for g in range(GROUPS):

            @pl.when((f >= k) & (f < nf - 1))
            def _():
                ag_copy(0, f - k, g).wait_send()

            @pl.when((f + k < nf) & (f > 0))
            def _():
                ag_copy(1, f + k, g).wait_send()


def place(*refs):
    sources, targets, held, (come, go) = refs[:4], refs[4:8], refs[8:12], refs[12:]
    pieces = [(i, 0, ref.shape[0]) for i, ref in enumerate(sources[:3])]
    rows = sources[3].shape[0] // 4
    pieces += [(3, rows * k, rows) for k in range(4)]
    loads, stores = [], []
    for n, (i, first, count) in enumerate(pieces):
        rows = pl.ds(first, count)
        loads.append(pltpu.make_async_copy(sources[i].at[rows], held[i].at[rows], come.at[n]))
        stores.append(pltpu.make_async_copy(held[i].at[rows], targets[i].at[rows], go.at[n]))
    for copy in loads:
        copy.start()
    for load, store in zip(loads, stores):
        load.wait()
        store.start()
    for copy in stores:
        copy.wait()


def per_device(master, moment_one, moment_two, grads, counts, step):
    nf = lax.axis_size("fsdp")
    rows = master.shape[2]
    vmem = pl.BlockSpec(memory_space=pltpu.VMEM)
    hbm = pl.BlockSpec(memory_space=pltpu.HBM)
    smem = pl.BlockSpec(memory_space=pltpu.SMEM)
    state = jax.ShapeDtypeStruct((rows, D), jnp.float32)
    wide_chunks = pltpu.VMEM((CHUNKS, 8, D), jnp.float32)
    short_chunks = pltpu.VMEM((CHUNKS, 16, HALF), jnp.int16)
    dma = pltpu.SemaphoreType.DMA
    results = pl.pallas_call(
        kernel,
        out_shape=(state, state, state, jax.ShapeDtypeStruct((nf * GROUPS, 16, HALF), jnp.bfloat16)),
        in_specs=[hbm] * 4 + [smem] * 2,
        out_specs=[hbm] * 4,
        scratch_shapes=[pltpu.VMEM((rows, D), jnp.float32)] * 3
        + [pltpu.VMEM((nf * GROUPS, 16, HALF), jnp.bfloat16), dma((CHUNKS,)), dma((nf * GROUPS,))]
        + [pltpu.VMEM((rows, D), jnp.float32)] * 4
        + [pltpu.VMEM((rows, D), jnp.bfloat16)]
        + [wide_chunks] * 4
        + [short_chunks] * 3
        + [pltpu.VMEM((6, 8, 128), jnp.float32)]
        + [dma((10,))]
        + [dma((2, CHUNKS))] * 2
        + [dma((CHUNKS,))] * 4
        + [dma((4,))] * 2
        + [dma((2, nf * GROUPS)), dma((nf * GROUPS,))],
        compiler_params=pltpu.CompilerParams(
            collective_id=0, has_side_effects=True, vmem_limit_bytes=60 << 20
        ),
    )(
        *(a.reshape(rows, D) for a in (master, moment_one, moment_two, grads)),
        counts.reshape(counts.shape[-1]),
        step,
    )
    results = (*results[:3], results[3].reshape(nf * GROUPS, 2, 8, HALF).transpose(0, 2, 1, 3).reshape(nf * rows, D))
    results = pl.pallas_call(
        place,
        out_shape=[jax.ShapeDtypeStruct(a.shape, a.dtype) for a in results],
        in_specs=[hbm] * 4,
        out_specs=[hbm] * 4,
        scratch_shapes=[pltpu.VMEM(a.shape, a.dtype) for a in results] + [dma((7,))] * 2,
        compiler_params=pltpu.CompilerParams(vmem_limit_bytes=60 << 20),
    )(*results)
    return (
        *(a.reshape(1, 1, rows, D) for a in results[:3]),
        results[3].reshape(1, 1, 1, nf * rows, D),
    )


def solution(mesh):
    split = P("row", "col", "fsdp", None)
    return jax.shard_map(
        per_device,
        mesh=mesh,
        in_specs=(split, split, split, split, P("row", "col", None), P()),
        out_specs=(split, split, split, P("row", "col", "fsdp", None, None)),
        check_vma=False,
    )
```
